512 devices in a mesh: sensor: 64 (over z, y), tm: 8 (over x, core).
Axes of the slice: x: 4, y: 4, z: 16, core: 2. Of those that a mesh axis runs over, the one named last changes fastest.
Arguments:
- signal: bfloat16 [64, 512, 8192], P(None, 'tm', 'sensor'), may hold values from -6 to 6
- conv_weight: bfloat16 [128, 128], replicated, may hold values from -0.5 to 0.5
- conv_bias: float32 [128], replicated, may hold values from -3 to 3
- diff_weight: bfloat16 [64, 192], replicated, may hold values from -1.5 to 1.5
- neighbour_index: int32 [8192, 32], P('sensor'), may hold values from 0 to 8191, as said below
- neighbour_count: int32 [8192], P('sensor'), may hold values from 2 to 32, as said below
- edge_weight: float32 [8192, 32], P('sensor'), may hold values from 0.05 to 10
- cotangent: bfloat16 [64, 512, 8192], P(None, 'tm', 'sensor'), may hold values from -6 to 6
Outputs:
- output: bfloat16 [64, 512, 8192], P(None, 'tm', 'sensor')
- grad_signal: bfloat16 [64, 512, 8192], P(None, 'tm', 'sensor')
The draws below stay inside these ranges and needn't reach their ends.
Inputs may be any that keep to these rules, and one draw needn't show every extreme that they name: `neighbour_index`: sensor s belongs to partition s // 128. The live slots of a sensor name distinct sensors other than itself. The sensors of one partition name at most 4 distinct sensors of any other partition in live slots, and at most 4 sensors of one partition have a live slot naming a sensor of any one other partition; in every draw some partition names exactly 4 sensors of every other partition. The live slots of a sensor are its first neighbour_count slots; some sensor of every partition has all 32 live.
All inputs are finite; a program needn't handle non-finite values.
Results may differ from the reference program's by a relative error of at most 0.0045.
Values may be sent and summed in bfloat16 or wider, within the bound.
No kernel may reach another device: no remote copies, remote signals or barrier semaphores. Data moves between devices by JAX's collectives and lax.ppermute only.
A program may use at most 128 MiB of HBM per device.

```python
import jax
import jax.numpy as jnp
from jax import lax

CHANNELS = 64
SLOTS = 32
DILATION = 8
CAPACITY = 4
SEN_DEV = 128
SENSORS = 8192
STEPS = 512


def graph_table(key):
    blocks = SENSORS // SEN_DEV
    far_count = (blocks * CAPACITY + SEN_DEV - 1) // SEN_DEV
    key_list = jax.random.split(jax.random.fold_in(key, 11), 5)
    fullest = jax.random.randint(key_list[0], (), 0, blocks)
    thinned = jax.random.randint(key_list[1], (blocks,), 1, blocks)
    peers = jnp.arange(blocks, dtype=jnp.int32)
    lighter = (peers + thinned) % blocks
    demand = jnp.where(peers[None, :] == lighter[:, None], CAPACITY - 1, CAPACITY)
    demand = jnp.where(peers[:, None] == fullest, CAPACITY, demand)
    demand = jnp.where(peers[:, None] == peers[None, :], 0, demand)
    pick_keys = jax.random.split(key_list[2], blocks * blocks)
    picks = jax.vmap(lambda subkey: jax.random.permutation(subkey, SEN_DEV)[:CAPACITY])(pick_keys)
    picks = picks.reshape(blocks, blocks, CAPACITY)
    order = jax.vmap(lambda subkey: jax.random.permutation(subkey, SEN_DEV))(jax.random.split(key_list[3], blocks))
    offsets = jax.vmap(lambda subkey: 1 + jax.random.permutation(subkey, SEN_DEV - 1)[:SLOTS])(jax.random.split(key_list[4], blocks))
    position = jnp.arange(SEN_DEV, dtype=jnp.int32)
    slot_ids = jnp.arange(SLOTS, dtype=jnp.int32)
    nearby = (order[:, :, None] + offsets[:, None, :]) % SEN_DEV + (peers * SEN_DEV)[:, None, None]
    grid = slot_ids[None, :] * SEN_DEV + position[:, None]
    peer_of = jnp.minimum(grid // CAPACITY, blocks - 1)
    column = grid % CAPACITY
    inside = (grid < blocks * CAPACITY) & (slot_ids[None, :] < far_count)
    wanted = demand[peers[:, None, None], peer_of[None]]
    linked = inside[None] & (peer_of[None] != peers[:, None, None]) & (column[None] < wanted)
    distant = peer_of[None] * SEN_DEV + picks[peers[:, None, None], peer_of[None], column[None]]
    table = jnp.where(linked, distant, nearby)
    inverse = jnp.argsort(order, axis=1)
    table = jnp.take_along_axis(table, inverse[:, :, None], axis=1)
    return table.reshape(blocks * SEN_DEV, SLOTS).astype(jnp.int32)


def draw_neighbour_index(key, part):
    return graph_table(key)


def draw_neighbour_count(key, part):
    blocks = SENSORS // SEN_DEV
    far_count = (blocks * CAPACITY + SEN_DEV - 1) // SEN_DEV
    key_list = jax.random.split(jax.random.fold_in(key, 23), 2)
    counts = jax.random.randint(key_list[0], (blocks, SEN_DEV), far_count, SLOTS + 1)
    widest = jax.random.randint(key_list[1], (blocks,), 0, SEN_DEV)
    counts = jnp.where(jnp.arange(SEN_DEV)[None, :] == widest[:, None], SLOTS, counts)
    return counts.reshape(blocks * SEN_DEV).astype(jnp.int32)


def draw_edge_weight(key, part):
    table = graph_table(key)
    key = jax.random.fold_in(key, 37)
    key_list = jax.random.split(key, 2)
    home = (jnp.arange(SENSORS, dtype=jnp.int32) // SEN_DEV)[:, None]
    across = table // SEN_DEV != home
    near_level = jax.random.uniform(key_list[0], (SENSORS, SLOTS), jnp.float32, jnp.log(0.05), jnp.log(1.0))
    far_level = jax.random.uniform(key_list[1], (SENSORS, SLOTS), jnp.float32, jnp.log(3.0), jnp.log(10.0))
    return jnp.exp(jnp.where(across, far_level, near_level)).astype(jnp.float32)


def block_scale(own_key, shape, pieces, low, top_value):
    loudness, own = 1.0, jax.random.fold_in(own_key, 6)
    for dim, blocks in pieces:
        heights = jnp.exp(jax.random.uniform(jax.random.fold_in(own, dim), (blocks,), jnp.float32, low / len(pieces), top_value / len(pieces)))
        loudness = loudness * jnp.repeat(heights, shape[dim] // blocks).reshape([-1 if axis == dim else 1 for axis in range(len(shape))])
    return loudness


def centred(rng, extent, deviation, most, shards=(), kind=jnp.bfloat16):
    result = deviation * jax.random.normal(rng, extent, jnp.float32)
    if shards:
        result = result * block_scale(rng, extent, shards, -0.22, 0.18)
    return jnp.clip(result, -most, most).astype(kind)


def setup_inputs(seed: int = 0) -> dict:
    streams_of = jax.random.split(jax.random.key(seed), 9)
    signal = centred(streams_of[0], (CHANNELS, STEPS, SENSORS), 1.0, 6.0, ((1, 8), (2, 64)))
    conv_weight = centred(streams_of[1], (2 * CHANNELS, 2 * CHANNELS), (2 * CHANNELS) ** -0.5, 0.5)
    conv_bias = centred(streams_of[2], (2 * CHANNELS,), 0.5, 3.0, (), jnp.float32)
    diff_weight = centred(streams_of[3], (CHANNELS, 3 * CHANNELS), (CHANNELS // 4) ** -0.5, 1.5)
    neighbour_index = draw_neighbour_index(jax.random.fold_in(streams_of[8], 71), 0)
    neighbour_count = draw_neighbour_count(jax.random.fold_in(streams_of[8], 71), 0)
    edge_weight = draw_edge_weight(jax.random.fold_in(streams_of[8], 71), 0)
    cotangent = centred(streams_of[7], (CHANNELS, STEPS, SENSORS), 1.0, 6.0, ((1, 8), (2, 64)))
    return dict(signal=signal, conv_weight=conv_weight, conv_bias=conv_bias, diff_weight=diff_weight, neighbour_index=neighbour_index, neighbour_count=neighbour_count, edge_weight=edge_weight, cotangent=cotangent)


def normalized(neighbour_count, edge_weight):
    live = jnp.arange(SLOTS, dtype=jnp.int32)[None, :] < neighbour_count[:, None]
    masked = jnp.where(live, edge_weight, jnp.float32(0.0))
    return (masked / jnp.sum(masked, axis=1, keepdims=True)).astype(jnp.bfloat16)


def spread(values, neighbour_index, trans):
    def add_slot(slot_index, total):
        targets = lax.dynamic_slice_in_dim(neighbour_index, slot_index, 1, 1)[:, 0]
        factor = lax.dynamic_slice_in_dim(trans, slot_index, 1, 1).astype(jnp.float32)
        return total + factor * values[targets].astype(jnp.float32)

    start = jnp.zeros(values.shape, jnp.float32)
    return lax.fori_loop(0, SLOTS, add_slot, start)


def spread_back(values, neighbour_index, trans):
    source = values.astype(jnp.float32)

    def add_slot(slot_index, total):
        targets = lax.dynamic_slice_in_dim(neighbour_index, slot_index, 1, 1)[:, 0]
        factor = lax.dynamic_slice_in_dim(trans, slot_index, 1, 1).astype(jnp.float32)
        return total.at[targets].add(factor * source)

    start = jnp.zeros(values.shape, jnp.float32)
    return lax.fori_loop(0, SLOTS, add_slot, start)


def to_rows(field):
    return field.reshape(CHANNELS * STEPS, SENSORS).T


def from_rows(field):
    return field.T.reshape(CHANNELS, STEPS * SENSORS)


def reference(signal, conv_weight, conv_bias, diff_weight, neighbour_index, neighbour_count, edge_weight, cotangent):
    trans = normalized(neighbour_count, edge_weight)
    lagged = jnp.concatenate([jnp.zeros((CHANNELS, DILATION, SENSORS), jnp.bfloat16), signal[:, :STEPS - DILATION, :]], axis=1)
    stacked = jnp.concatenate([lagged, signal], axis=0).reshape(2 * CHANNELS, STEPS * SENSORS)
    preact = jnp.dot(conv_weight, stacked, preferred_element_type=jnp.float32) + conv_bias[:, None]
    tanh_part = jnp.tanh(preact[:CHANNELS])
    gate_part = jax.nn.sigmoid(preact[CHANNELS:])
    hidden = (tanh_part * gate_part).astype(jnp.bfloat16)
    hop_one = from_rows(spread(to_rows(hidden), neighbour_index, trans)).astype(jnp.bfloat16)
    hop_two = from_rows(spread(to_rows(hop_one), neighbour_index, trans)).astype(jnp.bfloat16)
    mixed = jnp.dot(diff_weight, jnp.concatenate([hidden, hop_one, hop_two], axis=0), preferred_element_type=jnp.float32)
    output = (signal.reshape(CHANNELS, STEPS * SENSORS).astype(jnp.float32) + mixed).astype(jnp.bfloat16)
    output = output.reshape(CHANNELS, STEPS, SENSORS)
    grad_flat = cotangent.reshape(CHANNELS, STEPS * SENSORS)
    theta_back = jnp.dot(diff_weight.T, grad_flat, preferred_element_type=jnp.float32)
    second = theta_back[2 * CHANNELS:].astype(jnp.bfloat16)
    first = (theta_back[CHANNELS:2 * CHANNELS] + from_rows(spread_back(to_rows(second), neighbour_index, trans))).astype(jnp.bfloat16)
    grad_hidden = theta_back[:CHANNELS] + from_rows(spread_back(to_rows(first), neighbour_index, trans))
    grad_tanh = grad_hidden * gate_part * (1.0 - tanh_part * tanh_part)
    grad_gate = grad_hidden * tanh_part * gate_part * (1.0 - gate_part)
    grad_pre = jnp.concatenate([grad_tanh, grad_gate], axis=0).astype(jnp.bfloat16)
    conv_back = jnp.dot(conv_weight.T, grad_pre, preferred_element_type=jnp.float32)
    lag_back = conv_back[:CHANNELS].reshape(CHANNELS, STEPS, SENSORS)
    now_back = conv_back[CHANNELS:].reshape(CHANNELS, STEPS, SENSORS)
    shifted = jnp.concatenate([lag_back[:, DILATION:, :], jnp.zeros((CHANNELS, DILATION, SENSORS), jnp.float32)], axis=1)
    grad_signal = (cotangent.astype(jnp.float32) + now_back + shifted).astype(jnp.bfloat16)
    return output, grad_signal
```

```python
import functools

import jax
import jax.numpy as jnp
from jax import lax
from jax.experimental import pallas as pl
from jax.experimental.pallas import tpu as pltpu
from jax.sharding import PartitionSpec as P

DILATION = 8
CAPACITY = 4

ROWS_BY_ROWS = (((1,), (1,)), ((), ()))


def from_behind(value, axis, by):
    count = lax.axis_size(axis)
    pairs = [(i, i + by) for i in range(count) if 0 <= i + by < count]
    return lax.ppermute(value, axis, pairs)


def mm(left, right):
    return jnp.dot(left, right, preferred_element_type=jnp.float32)


def mm_t(left, right):
    return lax.dot_general(left, right, ROWS_BY_ROWS, preferred_element_type=jnp.float32)


def table_kernel(peers, me_ref, index_ref, count_ref, weight_ref, near_ref, far_ref, request_ref, member_all, owner_all):
    sensors, slots = index_ref.shape
    me = me_ref[0]
    index = index_ref[...].T
    live = lax.broadcasted_iota(jnp.int32, (slots, sensors), 0) < count_ref[...]
    masked = jnp.where(live, weight_ref[...].T, 0.0)
    trans = masked / jnp.sum(masked, axis=0, keepdims=True)
    trans = trans.astype(jnp.bfloat16).astype(jnp.float32)
    owner = jnp.where(live, index // sensors, -1)
    member = index % sensors
    member_ids = lax.broadcasted_iota(jnp.int32, (sensors, sensors), 0)
    owner_ids = lax.broadcasted_iota(jnp.int32, (peers, sensors), 0)
    near = jnp.zeros((sensors, sensors), jnp.float32)
    for j in range(slots):
        place = slice(j * sensors, (j + 1) * sensors)
        hit = member_ids == member[j : j + 1]
        member_all[:, place] = jnp.where(hit, 1.0, 0.0).astype(jnp.bfloat16)
        owner_all[:, place] = jnp.where(owner_ids == owner[j : j + 1], 1.0, 0.0).astype(jnp.bfloat16)
        home = jnp.where(owner[j : j + 1] == me, trans[j : j + 1], 0.0)
        near = near + jnp.where(hit, home, 0.0)
    near_ref[...] = near.astype(jnp.bfloat16)
    named = mm_t(owner_all[...], member_all[...])
    named = (named > 0.0) & (owner_ids != me)
    flags = jnp.where(named, 1.0, 0.0).astype(jnp.bfloat16)
    below = lax.broadcasted_iota(jnp.int32, (sensors, sensors), 0) < lax.broadcasted_iota(
        jnp.int32, (sensors, sensors), 1
    )
    rank = mm(flags, jnp.where(below, 1.0, 0.0).astype(jnp.bfloat16))
    rank = jnp.where(named, rank, 255.0).astype(jnp.bfloat16)
    places = peers * CAPACITY
    expand = lax.broadcasted_iota(jnp.int32, (places, peers), 0) // CAPACITY == lax.broadcasted_iota(
        jnp.int32, (places, peers), 1
    )
    rank = mm(jnp.where(expand, 1.0, 0.0).astype(jnp.bfloat16), rank)
    place_ids = lax.broadcasted_iota(jnp.int32, (places, sensors), 0)
    wanted_rank = (place_ids % CAPACITY).astype(jnp.float32)
    chosen = jnp.where(rank == wanted_rank, 1.0, 0.0).astype(jnp.bfloat16)
    lane_ids = lax.broadcasted_iota(jnp.int32, (8, sensors), 1).astype(jnp.float32)
    label = jnp.where(lax.broadcasted_iota(jnp.int32, (8, sensors), 0) == 0, lane_ids, 1.0).astype(jnp.bfloat16)
    asked = mm_t(label, chosen).astype(jnp.int32)
    request_ref[...] = jnp.where(asked[1:2] > 0, asked[0:1], -1)
    place_owner = place_ids // CAPACITY
    far = jnp.zeros((places, sensors), jnp.float32)
    for j in range(slots):
        found = mm(chosen, member_all[:, j * sensors : (j + 1) * sensors])
        far = far + jnp.where(place_owner == owner[j : j + 1], found * trans[j : j + 1], 0.0)
    far_ref[...] = far.astype(jnp.bfloat16)


def swap_requests(request, axis):
    count = lax.axis_size(axis)
    me = lax.axis_index(axis)
    width = request.shape[1]
    blocks = lax.dynamic_slice_in_dim(jnp.concatenate([request, request], axis=0), me, count, 0)
    step = 1
    while step < count:
        parts = blocks.reshape(count // (2 * step), 2, step * width)
        moved = lax.ppermute(parts[:, 1], axis, [(i, (i + step) % count) for i in range(count)])
        blocks = jnp.stack([parts[:, 0], moved], axis=1).reshape(count, width)
        step *= 2
    blocks = jnp.concatenate([blocks[:1], blocks[:0:-1]], axis=0)
    return lax.dynamic_slice_in_dim(jnp.concatenate([blocks, blocks], axis=0), count - me, count, 0)


def build_tables(peers, myself, index, count, weight):
    sensors, slots = index.shape
    places = peers * CAPACITY
    vmem = pl.BlockSpec(memory_space=pltpu.VMEM)
    return pl.pallas_call(
        functools.partial(table_kernel, peers),
        out_shape=(
            jax.ShapeDtypeStruct((sensors, sensors), jnp.bfloat16),
            jax.ShapeDtypeStruct((places, sensors), jnp.bfloat16),
            jax.ShapeDtypeStruct((1, places), jnp.int32),
        ),
        in_specs=[pl.BlockSpec(memory_space=pltpu.SMEM), vmem, vmem, vmem],
        out_specs=(vmem, vmem, vmem),
        scratch_shapes=[
            pltpu.VMEM((sensors, slots * sensors), jnp.bfloat16),
            pltpu.VMEM((peers, slots * sensors), jnp.bfloat16),
        ],
        compiler_params=pltpu.CompilerParams(vmem_limit_bytes=32 * 1024 * 1024),
        cost_estimate=pl.CostEstimate(flops=4 * 10**8, bytes_accessed=10**6, transcendentals=0),
        name="tables",
    )(myself.reshape(1).astype(jnp.int32), index, count.reshape(1, sensors), weight)


def per_device(
    signal,
    conv_weight,
    conv_bias,
    diff_weight,
    neighbour_index,
    neighbour_count,
    edge_weight,
    cotangent,
):
    channels, step_count, sensor_count = signal.shape
    row_count = channels * step_count
    peer_count = lax.axis_size("sensor")
    myself = lax.axis_index("sensor")
    near_t, far_t, request = build_tables(
        peer_count, myself, neighbour_index, neighbour_count, edge_weight
    )

    def exchange(pieces, earlier=None):
        shaped = pieces.astype(jnp.bfloat16).reshape(peer_count, CAPACITY, row_count)
        if earlier is not None:
            shaped, earlier = lax.optimization_barrier((shaped, earlier))
        return lax.all_to_all(shaped, "sensor", split_axis=0, concat_axis=0, tiled=True)

    def absorb(arrived, places):
        return lax.dot_general(
            arrived.reshape(peer_count * CAPACITY, row_count),
            places,
            (((0,), (0,)), ((), ())),
            preferred_element_type=jnp.float32,
        )

    grad_flat = cotangent.reshape(channels, step_count * sensor_count)
    theta_back = lax.dot_general(
        diff_weight, grad_flat, (((0,), (0,)), ((), ())), preferred_element_type=jnp.float32
    )
    second = theta_back[2 * channels :].astype(jnp.bfloat16).reshape(row_count, sensor_count)
    second_far = exchange(mm_t(far_t, second))

    asked = swap_requests(request.reshape(peer_count, CAPACITY), "sensor")
    pick = (asked[:, :, None] == lax.broadcasted_iota(jnp.int32, (1, 1, sensor_count), 2)).astype(jnp.bfloat16)
    pick = lax.optimization_barrier(pick.reshape(peer_count * CAPACITY, sensor_count))

    tail_steps = signal[:, step_count - DILATION :, :]
    before = from_behind(tail_steps, "tm", 1)
    lagged = jnp.concatenate([before, signal[:, : step_count - DILATION, :]], axis=1)
    stacked = jnp.concatenate([lagged, signal], axis=0).reshape(
        2 * channels, step_count * sensor_count
    )
    preact = mm(conv_weight, stacked) + conv_bias[:, None]
    tanh_part = jnp.tanh(preact[:channels])
    gate_part = jax.nn.sigmoid(preact[channels:])
    hidden = (tanh_part * gate_part).astype(jnp.bfloat16)
    hidden_rows = hidden.reshape(row_count, sensor_count)
    hidden_far = exchange(mm_t(pick, hidden_rows), second_far)

    first = theta_back[channels : 2 * channels] + (
        mm_t(second, near_t) + absorb(second_far, pick)
    ).reshape(channels, -1)
    first = first.astype(jnp.bfloat16).reshape(row_count, sensor_count)
    first_far = exchange(mm_t(far_t, first), hidden_far)

    hop_one = (mm(hidden_rows, near_t) + absorb(hidden_far, far_t)).astype(jnp.bfloat16)
    hop_far = exchange(mm_t(pick, hop_one), first_far)

    grad_hidden = theta_back[:channels] + (
        mm_t(first, near_t) + absorb(first_far, pick)
    ).reshape(channels, -1)
    grad_tanh = grad_hidden * gate_part * (1.0 - tanh_part * tanh_part)
    grad_gate = grad_hidden * tanh_part * gate_part * (1.0 - gate_part)
    grad_pre = jnp.concatenate([grad_tanh, grad_gate], axis=0).astype(jnp.bfloat16)
    conv_back = lax.dot_general(
        conv_weight, grad_pre, (((0,), (0,)), ((), ())), preferred_element_type=jnp.float32
    )
    lag_back = conv_back[:channels].reshape(channels, step_count, sensor_count)
    now_back = conv_back[channels:].reshape(channels, step_count, sensor_count)
    after = from_behind(lag_back[:, :DILATION, :].astype(jnp.bfloat16), "tm", -1).astype(
        jnp.float32
    )
    shifted = jnp.concatenate([lag_back[:, DILATION:, :], after], axis=1)
    grad_signal = (cotangent.astype(jnp.float32) + now_back + shifted).astype(jnp.bfloat16)

    hop_two = (mm(hop_one, near_t) + absorb(hop_far, far_t)).astype(jnp.bfloat16)
    joined = jnp.concatenate(
        [hidden, hop_one.reshape(channels, -1), hop_two.reshape(channels, -1)], axis=0
    )
    mixed = mm(diff_weight, joined)
    output = (signal.reshape(channels, -1).astype(jnp.float32) + mixed).astype(jnp.bfloat16)
    output = output.reshape(channels, step_count, sensor_count)
    return (output, grad_signal)


def solution(mesh):
    placed = (
        P(None, "tm", "sensor"),
        P(),
        P(),
        P(),
        P("sensor", None),
        P("sensor"),
        P("sensor", None),
        P(None, "tm", "sensor"),
    )
    return jax.shard_map(
        per_device,
        mesh=mesh,
        in_specs=placed,
        out_specs=(P(None, "tm", "sensor"), P(None, "tm", "sensor")),
        check_vma=False,
    )
```

```python
import functools

import jax
import jax.numpy as jnp
from jax import lax
from jax.experimental import pallas as pl
from jax.experimental.pallas import tpu as pltpu
from jax.sharding import PartitionSpec as P

DILATION = 8
CAPACITY = 4
LANES = 128
SHARE = 16

ROWS_BY_ROWS = (((1,), (1,)), ((), ()))
COLUMNS_BY_COLUMNS = (((0,), (0,)), ((), ()))
VMEM = pl.BlockSpec(memory_space=pltpu.VMEM)


def from_behind(value, axis, by):
    count = lax.axis_size(axis)
    pairs = [(i, i + by) for i in range(count) if 0 <= i + by < count]
    return lax.ppermute(value, axis, pairs)


def mm(left, right):
    return jnp.dot(left, right, preferred_element_type=jnp.float32)


def mm_t(left, right):
    return lax.dot_general(left, right, ROWS_BY_ROWS, preferred_element_type=jnp.float32)


def t_mm(left, right):
    return lax.dot_general(left, right, COLUMNS_BY_COLUMNS, preferred_element_type=jnp.float32)


def graph_kernel(peers, me_ref, index_ref, count_ref, weight_ref, graph_ref, member_all, owner_all):
    sensors, slots = index_ref.shape
    places = peers * CAPACITY
    half = (places + sensors) // 2
    me = me_ref[0]
    index = index_ref[...].T
    live = lax.broadcasted_iota(jnp.int32, (slots, sensors), 0) < count_ref[...]
    masked = jnp.where(live, weight_ref[...].T, 0.0)
    trans = masked / jnp.sum(masked, axis=0, keepdims=True)
    owner = jnp.where(live, index // sensors, -1)
    member = index % sensors
    member_ids = lax.broadcasted_iota(jnp.int32, (sensors, sensors), 0)
    owner_ids = lax.broadcasted_iota(jnp.int32, (peers, sensors), 0)
    for j in range(slots):
        place = slice(j * sensors, (j + 1) * sensors)
        hit = member_ids == member[j : j + 1]
        member_all[:, place] = jnp.where(hit, 1.0, 0.0).astype(jnp.bfloat16)
        owner_all[:, place] = jnp.where(owner_ids == owner[j : j + 1], 1.0, 0.0).astype(jnp.bfloat16)
    named = mm_t(owner_all[...], member_all[...])
    named = (named > 0.0) & (owner_ids != me)
    flags = jnp.where(named, 1.0, 0.0).astype(jnp.bfloat16)
    below = lax.broadcasted_iota(jnp.int32, (sensors, sensors), 0) < lax.broadcasted_iota(
        jnp.int32, (sensors, sensors), 1
    )
    rank = mm(flags, jnp.where(below, 1.0, 0.0).astype(jnp.bfloat16))
    spread_rank = jnp.where(named, rank, 255.0).astype(jnp.bfloat16)
    ranks = mm(rank.astype(jnp.bfloat16), member_all[...])
    ranks = jnp.where(owner_all[...] > 0, ranks, 0.0)
    ranks = jnp.sum(ranks, axis=0, keepdims=True)
    ranks = jnp.concatenate([ranks[:, j * sensors : (j + 1) * sensors] for j in range(slots)], axis=0)
    distant = owner * CAPACITY + ranks.astype(jnp.int32)
    row = jnp.where(owner == me, places + member, distant) - half
    row = jnp.where(live, row, half)
    graph_ref[...] = jnp.zeros(graph_ref.shape, jnp.bfloat16)
    graph_ref[0:slots, :] = row.astype(jnp.float32).astype(jnp.bfloat16)
    graph_ref[slots : 2 * slots, :] = trans.astype(jnp.bfloat16)
    expand = lax.broadcasted_iota(jnp.int32, (places, peers), 0) // CAPACITY == lax.broadcasted_iota(
        jnp.int32, (places, peers), 1
    )
    spread_rank = mm(jnp.where(expand, 1.0, 0.0).astype(jnp.bfloat16), spread_rank)
    wanted_rank = (lax.broadcasted_iota(jnp.int32, (places, sensors), 0) % CAPACITY).astype(jnp.float32)
    chosen = jnp.where(spread_rank == wanted_rank, 1.0, 0.0).astype(jnp.bfloat16)
    lane_ids = lax.broadcasted_iota(jnp.int32, (SHARE, sensors), 1).astype(jnp.float32)
    first_row = lax.broadcasted_iota(jnp.int32, (SHARE, sensors), 0) == 0
    label = jnp.where(first_row, lane_ids, 1.0).astype(jnp.bfloat16)
    asked = mm_t(label, chosen)
    asked = jnp.where(asked[1:2] > 0.5, asked[0:1], -1.0)
    asked = jnp.concatenate([asked[:, i * sensors : (i + 1) * sensors] for i in range(places // sensors)], axis=0)
    asked = jnp.concatenate([asked, jnp.zeros((SHARE - asked.shape[0], sensors), jnp.float32)], axis=0)
    graph_ref[2 * slots : 2 * slots + SHARE, :] = asked.astype(jnp.bfloat16)


def own_graph(peers, shares, myself, index, count, weight):
    sensors, slots = index.shape
    return pl.pallas_call(
        functools.partial(graph_kernel, peers),
        out_shape=jax.ShapeDtypeStruct((shares * SHARE, sensors), jnp.bfloat16),
        in_specs=[pl.BlockSpec(memory_space=pltpu.SMEM), VMEM, VMEM, VMEM],
        out_specs=VMEM,
        scratch_shapes=[
            pltpu.VMEM((sensors, slots * sensors), jnp.bfloat16),
            pltpu.VMEM((peers, slots * sensors), jnp.bfloat16),
        ],
        compiler_params=pltpu.CompilerParams(vmem_limit_bytes=32 * 1024 * 1024),
        cost_estimate=pl.CostEstimate(flops=4 * 10**8, bytes_accessed=10**6, transcendentals=0),
        name="own_graph",
    )(myself.reshape(1).astype(jnp.int32), index, count.reshape(1, sensors), weight)


def tables_kernel(slots, group, graph_ref, asked_ref, table_ref, pick_ref):
    rows, sensors = table_ref.shape[1:]
    places = rows - sensors
    chunk = 64
    for i in range(group):
        per_share = graph_ref.shape[2]
        codes = [graph_ref[j // per_share, i, j % per_share : j % per_share + 1, :].astype(jnp.float32) for j in range(slots)]
        weights = [
            graph_ref[(slots + j) // per_share, i, j % per_share : j % per_share + 1, :].astype(jnp.float32)
            for j in range(slots)
        ]
        for start in range(0, rows, chunk):
            ids = lax.broadcasted_iota(jnp.int32, (chunk, sensors), 0).astype(jnp.float32) + (start - rows // 2)
            total = jnp.zeros((chunk, sensors), jnp.float32)
            for j in range(slots):
                total = jnp.where(ids == codes[j], weights[j], total)
            table_ref[i, start : start + chunk, :] = total.astype(jnp.bfloat16)
        own_ids = lax.broadcasted_iota(jnp.int32, (sensors, places), 0).astype(jnp.float32)
        asked = asked_ref[i : i + 1, :]
        pick_ref[i] = jnp.where(own_ids == asked, 1.0, 0.0).astype(jnp.bfloat16)


def all_tables(slots, graph, asked):
    shares, peers, per_share, sensors = graph.shape
    places = asked.shape[1]
    group = 8
    return pl.pallas_call(
        functools.partial(tables_kernel, slots, group),
        grid=(peers // group,),
        out_shape=(
            jax.ShapeDtypeStruct((peers, places + sensors, sensors), jnp.bfloat16),
            jax.ShapeDtypeStruct((peers, sensors, places), jnp.bfloat16),
        ),
        in_specs=[
            pl.BlockSpec((shares, group, per_share, sensors), lambda i: (0, i, 0, 0)),
            pl.BlockSpec((group, places), lambda i: (i, 0)),
        ],
        out_specs=(
            pl.BlockSpec((group, places + sensors, sensors), lambda i: (i, 0, 0)),
            pl.BlockSpec((group, sensors, places), lambda i: (i, 0, 0)),
        ),
        compiler_params=pltpu.CompilerParams(vmem_limit_bytes=32 * 1024 * 1024),
        cost_estimate=pl.CostEstimate(flops=2 * 10**8, bytes_accessed=12 * 10**6, transcendentals=0),
        name="all_tables",
    )(graph, asked)


def swap_places(gathered, pair, left, right):
    count = left.shape[0]
    low = lax.broadcasted_iota(jnp.int32, left.shape, 0) % (2 * CAPACITY) < CAPACITY
    even = jnp.where(low, left, pltpu.roll(right, CAPACITY, 0))
    odd = jnp.where(low, pltpu.roll(left, count - CAPACITY, 0), right)
    at = pl.ds(pl.multiple_of(pair * 2 * CAPACITY, 2 * CAPACITY), 2 * CAPACITY)
    shape = (count // (2 * CAPACITY), 2 * CAPACITY, left.shape[1])
    gathered[:, 0, at, :] = even.reshape(shape)
    gathered[:, 1, at, :] = odd.reshape(shape)


def back_kernel(places, grad_ref, weight_ref, table_ref, pick_ref, out_ref, base, second, first, gathered):
    peers, channels, sensors = grad_ref.shape

    @pl.loop(0, peers)
    def _(p):
        theta = t_mm(grad_ref[p], weight_ref[...])
        base[p] = theta[:, :LANES]
        second[p] = theta[:, LANES:].astype(jnp.bfloat16)

    def hop(source, finish):
        @pl.loop(0, peers // 2)
        def _(pair):
            left = mm(table_ref[2 * pair, :places, :], source[2 * pair])
            right = mm(table_ref[2 * pair + 1, :places, :], source[2 * pair + 1])
            swap_places(gathered, pair, left, right)

        @pl.loop(0, peers // 2)
        def _(pair):
            for side in range(2):
                p = 2 * pair + side
                far = mm(pick_ref[p], gathered[pair, side].astype(jnp.bfloat16))
                finish(p, far + mm(table_ref[p, places:, :], source[p]))

    def keep_first(p, value):
        first[p] = (base[p] + value).astype(jnp.bfloat16)

    def keep_out(p, value):
        out_ref[p] = value.T[:channels].astype(jnp.bfloat16)

    hop(second, keep_first)
    hop(first, keep_out)


def forward_kernel(places, hidden_ref, unit_ref, one_ref, two_ref, table_ref, pick_ref, out_ref, start, middle, gathered):
    peers, channels, sensors = hidden_ref.shape

    @pl.loop(0, peers)
    def _(p):
        start[p] = t_mm(hidden_ref[p], unit_ref[...]).astype(jnp.bfloat16)

    def hop(source, finish):
        @pl.loop(0, peers // 2)
        def _(pair):
            left = t_mm(pick_ref[2 * pair], source[2 * pair])
            right = t_mm(pick_ref[2 * pair + 1], source[2 * pair + 1])
            swap_places(gathered, pair, left, right)

        @pl.loop(0, peers // 2)
        def _(pair):
            for side in range(2):
                p = 2 * pair + side
                far = t_mm(table_ref[p, :places, :], gathered[pair, side].astype(jnp.bfloat16))
                finish(p, (far + t_mm(table_ref[p, places:, :], source[p])).astype(jnp.bfloat16))

    def keep_middle(p, value):
        middle[p] = value

    def keep_out(p, value):
        mixed = mm_t(one_ref[...], middle[p]) + mm_t(two_ref[...], value)
        out_ref[p] = mixed.astype(jnp.bfloat16)

    hop(start, keep_middle)
    hop(middle, keep_out)


def to_lanes(block):
    return jnp.pad(block, ((0, 0), (0, LANES - block.shape[1])))


def back_hops(grad, diff_weight, table, pick):
    peers, channels, sensors = grad.shape
    places = pick.shape[2]
    weight = jnp.concatenate(
        [to_lanes(diff_weight[:, channels : 2 * channels]), to_lanes(diff_weight[:, 2 * channels :])], axis=1
    )
    return pl.pallas_call(
        functools.partial(back_kernel, places),
        out_shape=jax.ShapeDtypeStruct(grad.shape, jnp.bfloat16),
        in_specs=[VMEM] * 4,
        out_specs=VMEM,
        scratch_shapes=[
            pltpu.VMEM((peers, sensors, LANES), jnp.float32),
            pltpu.VMEM((peers, sensors, LANES), jnp.bfloat16),
            pltpu.VMEM((peers, sensors, LANES), jnp.bfloat16),
            pltpu.VMEM((peers // 2, 2, peers * CAPACITY, LANES), jnp.float32),
        ],
        compiler_params=pltpu.CompilerParams(vmem_limit_bytes=48 * 1024 * 1024),
        cost_estimate=pl.CostEstimate(flops=3 * 10**9, bytes_accessed=12 * 10**6, transcendentals=0),
        name="back_hops",
    )(grad, weight, table, pick)


def forward_hops(hidden, diff_weight, table, pick):
    peers, channels, sensors = hidden.shape
    places = pick.shape[2]
    unit = to_lanes(jnp.eye(channels, dtype=jnp.bfloat16))
    one = to_lanes(diff_weight[:, channels : 2 * channels])
    two = to_lanes(diff_weight[:, 2 * channels :])
    return pl.pallas_call(
        functools.partial(forward_kernel, places),
        out_shape=jax.ShapeDtypeStruct(hidden.shape, jnp.bfloat16),
        in_specs=[VMEM] * 6,
        out_specs=VMEM,
        scratch_shapes=[
            pltpu.VMEM((peers, sensors, LANES), jnp.bfloat16),
            pltpu.VMEM((peers, sensors, LANES), jnp.bfloat16),
            pltpu.VMEM((peers // 2, 2, peers * CAPACITY, LANES), jnp.float32),
        ],
        compiler_params=pltpu.CompilerParams(vmem_limit_bytes=48 * 1024 * 1024),
        cost_estimate=pl.CostEstimate(flops=3 * 10**9, bytes_accessed=12 * 10**6, transcendentals=0),
        name="forward_hops",
    )(hidden, unit, one, two, table, pick)


def exchange(blocks, earlier=None):
    if earlier is not None:
        blocks, earlier = lax.optimization_barrier((blocks, earlier))
    return lax.all_to_all(blocks, "sensor", split_axis=0, concat_axis=0, tiled=True)


def asked_of(graph, slots, peer_count):
    sensors = graph.shape[3]
    rows = graph[2 * slots // SHARE, :, : peer_count * CAPACITY // sensors, :]
    rows = rows.reshape(peer_count, peer_count, CAPACITY).transpose(1, 0, 2)
    return rows.reshape(peer_count, peer_count * CAPACITY).astype(jnp.float32)


def per_device(
    signal,
    conv_weight,
    conv_bias,
    diff_weight,
    neighbour_index,
    neighbour_count,
    edge_weight,
    cotangent,
):
    channels, step_count, sensor_count = signal.shape
    slots = neighbour_index.shape[1]
    peer_count = lax.axis_size("sensor")
    share_count = lax.axis_size("tm")

    graph = own_graph(
        peer_count, share_count, lax.axis_index("sensor"), neighbour_index, neighbour_count, edge_weight
    )
    share = lax.dynamic_slice_in_dim(graph, lax.axis_index("tm") * SHARE, SHARE, 0)
    share = exchange(jnp.broadcast_to(share[None], (peer_count, SHARE, sensor_count)))
    grad_in = exchange(cotangent.transpose(1, 0, 2), share)
    graphs = lax.all_gather(share, "tm", axis=0, tiled=False)
    table, pick = all_tables(slots, graphs, asked_of(graphs, slots, peer_count))

    tail_steps = signal[:, step_count - DILATION :, :]
    before = from_behind(tail_steps, "tm", 1)
    lagged = jnp.concatenate([before, signal[:, : step_count - DILATION, :]], axis=1)
    stacked = jnp.concatenate([lagged, signal], axis=0).reshape(
        2 * channels, step_count * sensor_count
    )
    preact = mm(conv_weight, stacked) + conv_bias[:, None]
    tanh_part = jnp.tanh(preact[:channels])
    gate_part = jax.nn.sigmoid(preact[channels:])
    hidden = (tanh_part * gate_part).astype(jnp.bfloat16)
    hidden_in = exchange(
        hidden.reshape(channels, step_count, sensor_count).transpose(1, 0, 2), grad_in
    )

    grad_out = exchange(back_hops(grad_in, diff_weight, table, pick), hidden_in)
    mixed_out = exchange(forward_hops(hidden_in, diff_weight, table, pick), grad_out)

    theta_back = lax.dot_general(
        diff_weight[:, :channels],
        cotangent.reshape(channels, -1),
        COLUMNS_BY_COLUMNS,
        preferred_element_type=jnp.float32,
    )
    grad_hidden = theta_back + grad_out.transpose(1, 0, 2).reshape(channels, -1).astype(jnp.float32)
    grad_tanh = grad_hidden * gate_part * (1.0 - tanh_part * tanh_part)
    grad_gate = grad_hidden * tanh_part * gate_part * (1.0 - gate_part)
    grad_pre = jnp.concatenate([grad_tanh, grad_gate], axis=0).astype(jnp.bfloat16)
    conv_back = lax.dot_general(
        conv_weight, grad_pre, COLUMNS_BY_COLUMNS, preferred_element_type=jnp.float32
    )
    lag_back = conv_back[:channels].reshape(channels, step_count, sensor_count)
    now_back = conv_back[channels:].reshape(channels, step_count, sensor_count)
    after = from_behind(lag_back[:, :DILATION, :].astype(jnp.bfloat16), "tm", -1).astype(
        jnp.float32
    )
    shifted = jnp.concatenate([lag_back[:, DILATION:, :], after], axis=1)
    grad_signal = (cotangent.astype(jnp.float32) + now_back + shifted).astype(jnp.bfloat16)

    kept = signal.astype(jnp.float32) + mm(diff_weight[:, :channels], hidden).reshape(signal.shape)
    output = (kept + mixed_out.transpose(1, 0, 2).astype(jnp.float32)).astype(jnp.bfloat16)
    return (output, grad_signal)


def solution(mesh):
    placed = (
        P(None, "tm", "sensor"),
        P(),
        P(),
        P(),
        P("sensor", None),
        P("sensor"),
        P("sensor", None),
        P(None, "tm", "sensor"),
    )
    return jax.shard_map(
        per_device,
        mesh=mesh,
        in_specs=placed,
        out_specs=(P(None, "tm", "sensor"), P(None, "tm", "sensor")),
        check_vma=False,
    )
```

```python
import functools

import jax
import jax.numpy as jnp
from jax import lax
from jax.experimental import pallas as pl
from jax.experimental.pallas import tpu as pltpu
from jax.sharding import PartitionSpec as P

DILATION = 8
CAPACITY = 4
LANES = 128
SHARE = 16

ROWS_BY_ROWS = (((1,), (1,)), ((), ()))
COLUMNS_BY_COLUMNS = (((0,), (0,)), ((), ()))
VMEM = pl.BlockSpec(memory_space=pltpu.VMEM)


def from_behind(value, axis, by):
    count = lax.axis_size(axis)
    pairs = [(i, i + by) for i in range(count) if 0 <= i + by < count]
    return lax.ppermute(value, axis, pairs)


def mm(left, right):
    return jnp.dot(left, right, preferred_element_type=jnp.float32)


def mm_t(left, right):
    return lax.dot_general(left, right, ROWS_BY_ROWS, preferred_element_type=jnp.float32)


def t_mm(left, right):
    return lax.dot_general(left, right, COLUMNS_BY_COLUMNS, preferred_element_type=jnp.float32)


def graph_kernel(peers, me_ref, index_ref, count_ref, weight_ref, graph_ref, member_all, owner_all):
    sensors, slots = index_ref.shape
    places = peers * CAPACITY
    half = (places + sensors) // 2
    me = me_ref[0]
    index = index_ref[...].T
    live = lax.broadcasted_iota(jnp.int32, (slots, sensors), 0) < count_ref[...]
    masked = jnp.where(live, weight_ref[...].T, 0.0)
    trans = masked / jnp.sum(masked, axis=0, keepdims=True)
    owner = jnp.where(live, index // sensors, -1)
    member = index % sensors
    member_ids = lax.broadcasted_iota(jnp.int32, (sensors, sensors), 0)
    owner_ids = lax.broadcasted_iota(jnp.int32, (peers, sensors), 0)
    for j in range(slots):
        place = slice(j * sensors, (j + 1) * sensors)
        hit = member_ids == member[j : j + 1]
        member_all[:, place] = jnp.where(hit, 1.0, 0.0).astype(jnp.bfloat16)
        owner_all[:, place] = jnp.where(owner_ids == owner[j : j + 1], 1.0, 0.0).astype(jnp.bfloat16)
    named = mm_t(owner_all[...], member_all[...])
    named = (named > 0.0) & (owner_ids != me)
    flags = jnp.where(named, 1.0, 0.0).astype(jnp.bfloat16)
    below = lax.broadcasted_iota(jnp.int32, (sensors, sensors), 0) < lax.broadcasted_iota(
        jnp.int32, (sensors, sensors), 1
    )
    rank = mm(flags, jnp.where(below, 1.0, 0.0).astype(jnp.bfloat16))
    spread_rank = jnp.where(named, rank, 255.0).astype(jnp.bfloat16)
    ranks = mm(rank.astype(jnp.bfloat16), member_all[...])
    ranks = jnp.where(owner_all[...] > 0, ranks, 0.0)
    ranks = jnp.sum(ranks, axis=0, keepdims=True)
    ranks = jnp.concatenate([ranks[:, j * sensors : (j + 1) * sensors] for j in range(slots)], axis=0)
    distant = owner * CAPACITY + ranks.astype(jnp.int32)
    row = jnp.where(owner == me, places + member, distant) - half
    row = jnp.where(live, row, half)
    graph_ref[...] = jnp.zeros(graph_ref.shape, jnp.bfloat16)
    graph_ref[0:slots, :] = row.astype(jnp.float32).astype(jnp.bfloat16)
    graph_ref[slots : 2 * slots, :] = trans.astype(jnp.bfloat16)
    expand = lax.broadcasted_iota(jnp.int32, (places, peers), 0) // CAPACITY == lax.broadcasted_iota(
        jnp.int32, (places, peers), 1
    )
    spread_rank = mm(jnp.where(expand, 1.0, 0.0).astype(jnp.bfloat16), spread_rank)
    wanted_rank = (lax.broadcasted_iota(jnp.int32, (places, sensors), 0) % CAPACITY).astype(jnp.float32)
    chosen = jnp.where(spread_rank == wanted_rank, 1.0, 0.0).astype(jnp.bfloat16)
    lane_ids = lax.broadcasted_iota(jnp.int32, (SHARE, sensors), 1).astype(jnp.float32)
    first_row = lax.broadcasted_iota(jnp.int32, (SHARE, sensors), 0) == 0
    label = jnp.where(first_row, lane_ids, 1.0).astype(jnp.bfloat16)
    asked = mm_t(label, chosen)
    asked = jnp.where(asked[1:2] > 0.5, asked[0:1], -1.0)
    asked = jnp.concatenate([asked[:, i * sensors : (i + 1) * sensors] for i in range(places // sensors)], axis=0)
    asked = jnp.concatenate([asked, jnp.zeros((SHARE - asked.shape[0], sensors), jnp.float32)], axis=0)
    graph_ref[2 * slots : 2 * slots + SHARE, :] = asked.astype(jnp.bfloat16)


def own_graph(peers, shares, myself, index, count, weight):
    sensors, slots = index.shape
    return pl.pallas_call(
        functools.partial(graph_kernel, peers),
        out_shape=jax.ShapeDtypeStruct((shares * SHARE, sensors), jnp.bfloat16),
        in_specs=[pl.BlockSpec(memory_space=pltpu.SMEM), VMEM, VMEM, VMEM],
        out_specs=VMEM,
        scratch_shapes=[
            pltpu.VMEM((sensors, slots * sensors), jnp.bfloat16),
            pltpu.VMEM((peers, slots * sensors), jnp.bfloat16),
        ],
        compiler_params=pltpu.CompilerParams(vmem_limit_bytes=32 * 1024 * 1024),
        cost_estimate=pl.CostEstimate(flops=4 * 10**8, bytes_accessed=10**6, transcendentals=0),
        name="own_graph",
    )(myself.reshape(1).astype(jnp.int32), index, count.reshape(1, sensors), weight)


def tables_kernel(slots, group, graph_ref, asked_ref, table_ref, pick_ref):
    rows, sensors = table_ref.shape[1:]
    places = rows - sensors
    chunk = 128
    for i in range(group):
        per_share = graph_ref.shape[2]
        codes = [graph_ref[j // per_share, i, j % per_share : j % per_share + 1, :] for j in range(slots)]
        weights = [graph_ref[(slots + j) // per_share, i, j % per_share : j % per_share + 1, :] for j in range(slots)]
        for start in range(0, rows, chunk):
            ids = lax.broadcasted_iota(jnp.int32, (chunk, sensors), 0).astype(jnp.float32) + (start - rows // 2)
            ids = ids.astype(jnp.bfloat16)
            total = jnp.zeros((chunk, sensors), jnp.bfloat16)
            for j in range(slots):
                total = jnp.where(ids == codes[j], weights[j], total)
            table_ref[i, start : start + chunk, :] = total
        own_ids = lax.broadcasted_iota(jnp.int32, (sensors, places), 0).astype(jnp.float32).astype(jnp.bfloat16)
        asked = asked_ref[i : i + 1, :].astype(jnp.bfloat16)
        one = jnp.ones((sensors, places), jnp.bfloat16)
        pick_ref[i] = jnp.where(own_ids == asked, one, jnp.zeros_like(one))


def all_tables(slots, graph, asked):
    shares, peers, per_share, sensors = graph.shape
    places = asked.shape[1]
    group = 8
    return pl.pallas_call(
        functools.partial(tables_kernel, slots, group),
        grid=(peers // group,),
        out_shape=(
            jax.ShapeDtypeStruct((peers, places + sensors, sensors), jnp.bfloat16),
            jax.ShapeDtypeStruct((peers, sensors, places), jnp.bfloat16),
        ),
        in_specs=[
            pl.BlockSpec((shares, group, per_share, sensors), lambda i: (0, i, 0, 0)),
            pl.BlockSpec((group, places), lambda i: (i, 0)),
        ],
        out_specs=(
            pl.BlockSpec((group, places + sensors, sensors), lambda i: (i, 0, 0)),
            pl.BlockSpec((group, sensors, places), lambda i: (i, 0, 0)),
        ),
        compiler_params=pltpu.CompilerParams(vmem_limit_bytes=32 * 1024 * 1024),
        cost_estimate=pl.CostEstimate(flops=2 * 10**8, bytes_accessed=12 * 10**6, transcendentals=0),
        name="all_tables",
    )(graph, asked)


def swap_places(gathered, pair, left, right):
    count = left.shape[0]
    low = lax.broadcasted_iota(jnp.int32, left.shape, 0) % (2 * CAPACITY) < CAPACITY
    even = jnp.where(low, left, pltpu.roll(right, CAPACITY, 0))
    odd = jnp.where(low, pltpu.roll(left, count - CAPACITY, 0), right)
    at = pl.ds(pl.multiple_of(pair * 2 * CAPACITY, 2 * CAPACITY), 2 * CAPACITY)
    shape = (count // (2 * CAPACITY), 2 * CAPACITY, left.shape[1])
    gathered[:, 0, at, :] = even.reshape(shape)
    gathered[:, 1, at, :] = odd.reshape(shape)


def back_kernel(places, grad_ref, weight_ref, table_ref, pick_ref, out_ref, base, second, first, gathered):
    peers, channels, sensors = grad_ref.shape

    @pl.loop(0, peers, unroll=8)
    def _(p):
        theta = t_mm(grad_ref[p], weight_ref[...])
        base[p] = theta[:, :LANES]
        second[p] = theta[:, LANES:].astype(jnp.bfloat16)

    def hop(source, finish):
        @pl.loop(0, peers // 2, unroll=4)
        def _(pair):
            left = mm(table_ref[2 * pair, :places, :], source[2 * pair])
            right = mm(table_ref[2 * pair + 1, :places, :], source[2 * pair + 1])
            swap_places(gathered, pair, left, right)

        @pl.loop(0, peers // 2, unroll=4)
        def _(pair):
            for side in range(2):
                p = 2 * pair + side
                far = mm(pick_ref[p], gathered[pair, side].astype(jnp.bfloat16))
                finish(p, far + mm(table_ref[p, places:, :], source[p]))

    def keep_first(p, value):
        first[p] = (base[p] + value).astype(jnp.bfloat16)

    def keep_out(p, value):
        out_ref[p] = value.T[:channels].astype(jnp.bfloat16)

    hop(second, keep_first)
    hop(first, keep_out)


def forward_kernel(places, hidden_ref, unit_ref, one_ref, two_ref, table_ref, pick_ref, out_ref, start, middle, gathered):
    peers, channels, sensors = hidden_ref.shape

    @pl.loop(0, peers, unroll=8)
    def _(p):
        start[p] = t_mm(hidden_ref[p], unit_ref[...]).astype(jnp.bfloat16)

    def hop(source, finish):
        @pl.loop(0, peers // 2, unroll=4)
        def _(pair):
            left = t_mm(pick_ref[2 * pair], source[2 * pair])
            right = t_mm(pick_ref[2 * pair + 1], source[2 * pair + 1])
            swap_places(gathered, pair, left, right)

        @pl.loop(0, peers // 2, unroll=4)
        def _(pair):
            for side in range(2):
                p = 2 * pair + side
                far = t_mm(table_ref[p, :places, :], gathered[pair, side].astype(jnp.bfloat16))
                finish(p, (far + t_mm(table_ref[p, places:, :], source[p])).astype(jnp.bfloat16))

    def keep_middle(p, value):
        middle[p] = value

    def keep_out(p, value):
        mixed = mm_t(one_ref[...], middle[p]) + mm_t(two_ref[...], value)
        out_ref[p] = mixed.astype(jnp.bfloat16)

    hop(start, keep_middle)
    hop(middle, keep_out)


def to_lanes(block):
    return jnp.pad(block, ((0, 0), (0, LANES - block.shape[1])))


def back_hops(grad, diff_weight, table, pick):
    peers, channels, sensors = grad.shape
    places = pick.shape[2]
    weight = jnp.concatenate(
        [to_lanes(diff_weight[:, channels : 2 * channels]), to_lanes(diff_weight[:, 2 * channels :])], axis=1
    )
    return pl.pallas_call(
        functools.partial(back_kernel, places),
        out_shape=jax.ShapeDtypeStruct(grad.shape, jnp.bfloat16),
        in_specs=[VMEM] * 4,
        out_specs=VMEM,
        scratch_shapes=[
            pltpu.VMEM((peers, sensors, LANES), jnp.float32),
            pltpu.VMEM((peers, sensors, LANES), jnp.bfloat16),
            pltpu.VMEM((peers, sensors, LANES), jnp.bfloat16),
            pltpu.VMEM((peers // 2, 2, peers * CAPACITY, LANES), jnp.float32),
        ],
        compiler_params=pltpu.CompilerParams(vmem_limit_bytes=48 * 1024 * 1024),
        cost_estimate=pl.CostEstimate(flops=3 * 10**9, bytes_accessed=12 * 10**6, transcendentals=0),
        name="back_hops",
    )(grad, weight, table, pick)


def forward_hops(hidden, diff_weight, table, pick):
    peers, channels, sensors = hidden.shape
    places = pick.shape[2]
    unit = to_lanes(jnp.eye(channels, dtype=jnp.bfloat16))
    one = to_lanes(diff_weight[:, channels : 2 * channels])
    two = to_lanes(diff_weight[:, 2 * channels :])
    return pl.pallas_call(
        functools.partial(forward_kernel, places),
        out_shape=jax.ShapeDtypeStruct(hidden.shape, jnp.bfloat16),
        in_specs=[VMEM] * 6,
        out_specs=VMEM,
        scratch_shapes=[
            pltpu.VMEM((peers, sensors, LANES), jnp.bfloat16),
            pltpu.VMEM((peers, sensors, LANES), jnp.bfloat16),
            pltpu.VMEM((peers // 2, 2, peers * CAPACITY, LANES), jnp.float32),
        ],
        compiler_params=pltpu.CompilerParams(vmem_limit_bytes=48 * 1024 * 1024),
        cost_estimate=pl.CostEstimate(flops=3 * 10**9, bytes_accessed=12 * 10**6, transcendentals=0),
        name="forward_hops",
    )(hidden, unit, one, two, table, pick)


def exchange(blocks, earlier=None):
    if earlier is not None:
        blocks, earlier = lax.optimization_barrier((blocks, earlier))
    return lax.all_to_all(blocks, "sensor", split_axis=0, concat_axis=0, tiled=True)


def asked_of(graph, slots, peer_count):
    sensors = graph.shape[3]
    per_share = graph.shape[2]
    at = 2 * slots % per_share
    rows = graph[2 * slots // per_share, :, at : at + peer_count * CAPACITY // sensors, :]
    rows = rows.reshape(peer_count, peer_count, CAPACITY).transpose(1, 0, 2)
    return rows.reshape(peer_count, peer_count * CAPACITY).astype(jnp.float32)


def per_device(
    signal,
    conv_weight,
    conv_bias,
    diff_weight,
    neighbour_index,
    neighbour_count,
    edge_weight,
    cotangent,
):
    channels, step_count, sensor_count = signal.shape
    slots = neighbour_index.shape[1]
    peer_count = lax.axis_size("sensor")
    share_count = lax.axis_size("tm")

    graph = own_graph(
        peer_count, share_count, lax.axis_index("sensor"), neighbour_index, neighbour_count, edge_weight
    )
    share = lax.dynamic_slice_in_dim(graph, lax.axis_index("tm") * SHARE, SHARE, 0)
    share = exchange(jnp.broadcast_to(share[None], (peer_count, SHARE, sensor_count)))
    grad_in = exchange(cotangent.transpose(1, 0, 2), share)
    graphs = lax.all_gather(share, "tm", axis=0, tiled=False)
    table, pick = all_tables(slots, graphs, asked_of(graphs, slots, peer_count))

    tail_steps = signal[:, step_count - DILATION :, :]
    before = from_behind(tail_steps, "tm", 1)
    lagged = jnp.concatenate([before, signal[:, : step_count - DILATION, :]], axis=1)
    stacked = jnp.concatenate([lagged, signal], axis=0).reshape(
        2 * channels, step_count * sensor_count
    )
    preact = mm(conv_weight, stacked) + conv_bias[:, None]
    tanh_part = jnp.tanh(preact[:channels])
    gate_part = jax.nn.sigmoid(preact[channels:])
    hidden = (tanh_part * gate_part).astype(jnp.bfloat16)
    hidden_in = exchange(
        hidden.reshape(channels, step_count, sensor_count).transpose(1, 0, 2), grad_in
    )

    grad_out = exchange(back_hops(grad_in, diff_weight, table, pick), hidden_in)
    mixed_out = exchange(forward_hops(hidden_in, diff_weight, table, pick), grad_out)

    theta_back = lax.dot_general(
        diff_weight[:, :channels],
        cotangent.reshape(channels, -1),
        COLUMNS_BY_COLUMNS,
        preferred_element_type=jnp.float32,
    )
    grad_hidden = theta_back + grad_out.transpose(1, 0, 2).reshape(channels, -1).astype(jnp.float32)
    grad_tanh = grad_hidden * gate_part * (1.0 - tanh_part * tanh_part)
    grad_gate = grad_hidden * tanh_part * gate_part * (1.0 - gate_part)
    grad_pre = jnp.concatenate([grad_tanh, grad_gate], axis=0).astype(jnp.bfloat16)
    conv_back = lax.dot_general(
        conv_weight, grad_pre, COLUMNS_BY_COLUMNS, preferred_element_type=jnp.float32
    )
    lag_back = conv_back[:channels].reshape(channels, step_count, sensor_count)
    now_back = conv_back[channels:].reshape(channels, step_count, sensor_count)
    after = from_behind(lag_back[:, :DILATION, :].astype(jnp.bfloat16), "tm", -1).astype(
        jnp.float32
    )
    shifted = jnp.concatenate([lag_back[:, DILATION:, :], after], axis=1)
    grad_signal = (cotangent.astype(jnp.float32) + now_back + shifted).astype(jnp.bfloat16)

    kept = signal.astype(jnp.float32) + mm(diff_weight[:, :channels], hidden).reshape(signal.shape)
    output = (kept + mixed_out.transpose(1, 0, 2).astype(jnp.float32)).astype(jnp.bfloat16)
    return (output, grad_signal)


def solution(mesh):
    placed = (
        P(None, "tm", "sensor"),
        P(),
        P(),
        P(),
        P("sensor", None),
        P("sensor"),
        P("sensor", None),
        P(None, "tm", "sensor"),
    )
    return jax.shard_map(
        per_device,
        mesh=mesh,
        in_specs=placed,
        out_specs=(P(None, "tm", "sensor"), P(None, "tm", "sensor")),
        check_vma=False,
    )
```

```python
import functools

import jax
import jax.numpy as jnp
from jax import lax
from jax.experimental import pallas as pl
from jax.experimental.pallas import tpu as pltpu
from jax.sharding import PartitionSpec as P

DILATION = 8
CAPACITY = 4
LANES = 128
SUBLANES = 8

ROWS_BY_ROWS = (((1,), (1,)), ((), ()))
COLUMNS_BY_COLUMNS = (((0,), (0,)), ((), ()))
VMEM = pl.BlockSpec(memory_space=pltpu.VMEM)


def from_behind(value, axis, by):
    count = lax.axis_size(axis)
    pairs = [(i, i + by) for i in range(count) if 0 <= i + by < count]
    return lax.ppermute(value, axis, pairs)


def mm(left, right):
    return jnp.dot(left, right, preferred_element_type=jnp.float32)


def mm_t(left, right):
    return lax.dot_general(left, right, ROWS_BY_ROWS, preferred_element_type=jnp.float32)


def t_mm(left, right):
    return lax.dot_general(left, right, COLUMNS_BY_COLUMNS, preferred_element_type=jnp.float32)


def graph_kernel(peers, me_ref, index_ref, count_ref, weight_ref, graph_ref, member_all, owner_all, rows_all):
    slots, sensors = index_ref.shape
    places = peers * CAPACITY
    half = (places + sensors) // 2
    me = me_ref[0]
    index = index_ref[...]
    live = lax.broadcasted_iota(jnp.int32, (slots, sensors), 0) < count_ref[...]
    masked = jnp.where(live, weight_ref[...], 0.0)
    trans = masked / jnp.sum(masked, axis=0, keepdims=True)
    owner = jnp.where(live, index // sensors, -1)
    member = index % sensors
    member_ids = lax.broadcasted_iota(jnp.int32, (sensors, sensors), 0)
    owner_ids = lax.broadcasted_iota(jnp.int32, (peers, sensors), 0)
    for j in range(slots):
        place = slice(j * sensors, (j + 1) * sensors)
        hit = member_ids == member[j : j + 1]
        member_all[:, place] = jnp.where(hit, 1.0, 0.0).astype(jnp.bfloat16)
        owner_all[:, place] = jnp.where(owner_ids == owner[j : j + 1], 1.0, 0.0).astype(jnp.bfloat16)
    named = mm_t(owner_all[...], member_all[...])
    named = (named > 0.0) & (owner_ids != me)
    flags = jnp.where(named, 1.0, 0.0).astype(jnp.bfloat16)
    below = lax.broadcasted_iota(jnp.int32, (sensors, sensors), 0) < lax.broadcasted_iota(
        jnp.int32, (sensors, sensors), 1
    )
    rank = mm(flags, jnp.where(below, 1.0, 0.0).astype(jnp.bfloat16))
    spread_rank = jnp.where(named, rank, 255.0).astype(jnp.bfloat16)
    ranks = mm(rank.astype(jnp.bfloat16), member_all[...])
    ranks = jnp.where(owner_all[...] > 0, ranks, 0.0)
    ranks = jnp.sum(ranks, axis=0, keepdims=True)
    ranks = jnp.concatenate([ranks[:, j * sensors : (j + 1) * sensors] for j in range(slots)], axis=0)
    distant = owner * CAPACITY + ranks.astype(jnp.int32)
    row = jnp.where(owner == me, places + member, distant) - half
    row = jnp.where(live, row, half)
    row = row.astype(jnp.float32)
    trans = trans.astype(jnp.bfloat16).astype(jnp.float32)
    part = SUBLANES // 2
    for i in range(slots // part):
        rows_all[i] = jnp.concatenate([row[i * part : (i + 1) * part], trans[i * part : (i + 1) * part]], axis=0)
    expand = lax.broadcasted_iota(jnp.int32, (places, peers), 0) // CAPACITY == lax.broadcasted_iota(
        jnp.int32, (places, peers), 1
    )
    spread_rank = mm(jnp.where(expand, 1.0, 0.0).astype(jnp.bfloat16), spread_rank)
    wanted_rank = (lax.broadcasted_iota(jnp.int32, (places, sensors), 0) % CAPACITY).astype(jnp.float32)
    chosen = jnp.where(spread_rank == wanted_rank, 1.0, 0.0).astype(jnp.bfloat16)
    lane_ids = lax.broadcasted_iota(jnp.int32, (SUBLANES, sensors), 1).astype(jnp.float32)
    first_row = lax.broadcasted_iota(jnp.int32, (SUBLANES, sensors), 0) == 0
    label = jnp.where(first_row, lane_ids, 1.0).astype(jnp.bfloat16)
    asked = mm_t(label, chosen)
    asked = jnp.where(asked[1:2] > 0.5, asked[0:1], -1.0)
    asked = [asked[:, i * sensors : (i + 1) * sensors] for i in range(places // sensors)]
    asked.append(jnp.zeros((SUBLANES - len(asked), sensors), jnp.float32))
    graph_ref[...] = jnp.concatenate([rows_all[me_ref[1]]] + asked, axis=0).astype(jnp.bfloat16)


def own_graph(peers, myself, share, index, count, weight):
    sensors, slots = index.shape
    return pl.pallas_call(
        functools.partial(graph_kernel, peers),
        out_shape=jax.ShapeDtypeStruct((2 * SUBLANES, sensors), jnp.bfloat16),
        in_specs=[pl.BlockSpec(memory_space=pltpu.SMEM), VMEM, VMEM, VMEM],
        out_specs=VMEM,
        scratch_shapes=[
            pltpu.VMEM((sensors, slots * sensors), jnp.bfloat16),
            pltpu.VMEM((peers, slots * sensors), jnp.bfloat16),
            pltpu.VMEM((2 * slots // SUBLANES, SUBLANES, sensors), jnp.float32),
        ],
        compiler_params=pltpu.CompilerParams(vmem_limit_bytes=32 * 1024 * 1024),
        cost_estimate=pl.CostEstimate(flops=4 * 10**8, bytes_accessed=10**6, transcendentals=0),
        name="own_graph",
    )(jnp.stack([myself, share]).astype(jnp.int32), index.T, count.reshape(1, sensors), weight.T)


def fill_tables(p, shares, asked_ref, table_ref, pick_ref):
    rows, sensors = table_ref.shape[1:]
    places = rows - sensors
    part = SUBLANES // 2
    chunk = 128
    codes = [share[j : j + 1, :] for share in shares for j in range(part)]
    weights = [share[part + j : part + j + 1, :] for share in shares for j in range(part)]
    blocks = []
    for start in range(0, rows, chunk):
        ids = lax.broadcasted_iota(jnp.int32, (chunk, sensors), 0).astype(jnp.float32) + (start - rows // 2)
        ids = ids.astype(jnp.bfloat16)
        total = jnp.zeros((chunk, sensors), jnp.bfloat16)
        for code, weight in zip(codes, weights):
            total = jnp.where(ids == code, weight, total)
        table_ref[p, start : start + chunk, :] = total
        blocks.append(total)
    own_ids = lax.broadcasted_iota(jnp.int32, (sensors, places), 0).astype(jnp.float32).astype(jnp.bfloat16)
    asked = asked_ref[pl.ds(p, 1), :].astype(jnp.bfloat16)
    one = jnp.ones((sensors, places), jnp.bfloat16)
    pick_ref[p] = jnp.where(own_ids == asked, one, jnp.zeros_like(one))
    return blocks[: places // chunk]


def turn_requests(requests, asked_ref):
    peers, sublanes, lanes = requests.shape
    places = peers * CAPACITY
    rows = lax.broadcasted_iota(jnp.int32, requests.shape, 1)
    parts = [jnp.sum(jnp.where(rows == i, requests, 0.0), axis=1) for i in range(places // lanes)]
    named = jnp.concatenate(parts, axis=1).astype(jnp.bfloat16)
    peer_ids = lax.broadcasted_iota(jnp.int32, (peers, places), 0)
    owner = lax.broadcasted_iota(jnp.int32, (peers, places), 1) // CAPACITY
    belongs = jnp.where(peer_ids == owner, 1.0, 0.0).astype(jnp.bfloat16)
    every = t_mm(named, belongs)
    same = lax.broadcasted_iota(jnp.int32, (places, places), 0) % CAPACITY
    same = same == lax.broadcasted_iota(jnp.int32, (places, places), 1) % CAPACITY
    asked_ref[...] = mm(belongs, jnp.where(same, every, 0.0).astype(jnp.bfloat16))


def swap_places(gathered, pair, left, right):
    count = left.shape[0]
    low = lax.broadcasted_iota(jnp.int32, left.shape, 0) % (2 * CAPACITY) < CAPACITY
    even = jnp.where(low, left, pltpu.roll(right, CAPACITY, 0))
    odd = jnp.where(low, pltpu.roll(left, count - CAPACITY, 0), right)
    at = pl.ds(pl.multiple_of(pair * 2 * CAPACITY, 2 * CAPACITY), 2 * CAPACITY)
    shape = (count // (2 * CAPACITY), 2 * CAPACITY, left.shape[1])
    gathered[:, 0, at, :] = even.reshape(shape)
    gathered[:, 1, at, :] = odd.reshape(shape)


def back_kernel(
    places, arrived_ref, near_ref, far_ref, weight_ref, out_ref, table_ref, pick_ref, base, second, first, gathered, asked
):
    peers, channels, sensors = out_ref.shape
    start = channels + SUBLANES
    turn_requests(arrived_ref[:, start : start + SUBLANES, :].astype(jnp.float32), asked)

    @pl.loop(0, peers // 2, unroll=4)
    def _(pair):
        sent = []
        for side in range(2):
            p = 2 * pair + side
            theta = t_mm(arrived_ref[p, :channels, :], weight_ref[...])
            base[p] = theta[:, :LANES]
            value = theta[:, LANES:].astype(jnp.bfloat16)
            second[p] = value
            shares = [arrived_ref[p, channels:start, :]]
            shares += [near_ref[i, p] for i in range(near_ref.shape[0])]
            shares += [far_ref[i, p] for i in range(far_ref.shape[0])]
            blocks = fill_tables(p, shares, asked, table_ref, pick_ref)
            sent.append(jnp.concatenate([mm(block, value) for block in blocks], axis=0))
        swap_places(gathered, pair, *sent)

    def absorb(source, finish):
        @pl.loop(0, peers // 2, unroll=32)
        def _(pair):
            for side in range(2):
                p = 2 * pair + side
                far = mm(pick_ref[p], gathered[pair, side].astype(jnp.bfloat16))
                finish(p, far + mm(table_ref[p, places:, :], source[p]))

    def keep_first(p, value):
        first[p] = (base[p] + value).astype(jnp.bfloat16)

    def keep_out(p, value):
        out_ref[p] = value.T[:channels].astype(jnp.bfloat16)

    absorb(second, keep_first)

    @pl.loop(0, peers // 2, unroll=32)
    def _(pair):
        left = mm(table_ref[2 * pair, :places, :], first[2 * pair])
        right = mm(table_ref[2 * pair + 1, :places, :], first[2 * pair + 1])
        swap_places(gathered, pair, left, right)

    absorb(first, keep_out)


def forward_kernel(places, hidden_ref, unit_ref, one_ref, two_ref, table_ref, pick_ref, out_ref, start, middle, gathered):
    peers, channels, sensors = hidden_ref.shape

    @pl.loop(0, peers, unroll=32)
    def _(p):
        start[p] = t_mm(hidden_ref[p], unit_ref[...]).astype(jnp.bfloat16)

    def hop(source, finish):
        @pl.loop(0, peers // 2, unroll=32)
        def _(pair):
            left = t_mm(pick_ref[2 * pair], source[2 * pair])
            right = t_mm(pick_ref[2 * pair + 1], source[2 * pair + 1])
            swap_places(gathered, pair, left, right)

        @pl.loop(0, peers // 2, unroll=32)
        def _(pair):
            for side in range(2):
                p = 2 * pair + side
                far = t_mm(table_ref[p, :places, :], gathered[pair, side].astype(jnp.bfloat16))
                finish(p, (far + t_mm(table_ref[p, places:, :], source[p])).astype(jnp.bfloat16))

    def keep_middle(p, value):
        middle[p] = value

    def keep_out(p, value):
        mixed = mm_t(one_ref[...], middle[p]) + mm_t(two_ref[...], value)
        out_ref[p] = mixed.astype(jnp.bfloat16)

    hop(start, keep_middle)
    hop(middle, keep_out)


def to_lanes(block):
    return jnp.pad(block, ((0, 0), (0, LANES - block.shape[1])))


def back_hops(arrived, near, far, diff_weight):
    peers, _, sensors = arrived.shape
    channels = diff_weight.shape[0]
    places = peers * CAPACITY
    weight = jnp.concatenate(
        [to_lanes(diff_weight[:, channels : 2 * channels]), to_lanes(diff_weight[:, 2 * channels :])], axis=1
    )
    return pl.pallas_call(
        functools.partial(back_kernel, places),
        out_shape=(
            jax.ShapeDtypeStruct((peers, channels, sensors), jnp.bfloat16),
            jax.ShapeDtypeStruct((peers, places + sensors, sensors), jnp.bfloat16),
            jax.ShapeDtypeStruct((peers, sensors, places), jnp.bfloat16),
        ),
        in_specs=[VMEM] * 4,
        out_specs=(VMEM, VMEM, VMEM),
        scratch_shapes=[
            pltpu.VMEM((peers, sensors, LANES), jnp.float32),
            pltpu.VMEM((peers, sensors, LANES), jnp.bfloat16),
            pltpu.VMEM((peers, sensors, LANES), jnp.bfloat16),
            pltpu.VMEM((peers // 2, 2, peers * CAPACITY, LANES), jnp.float32),
            pltpu.VMEM((peers, places), jnp.float32),
        ],
        compiler_params=pltpu.CompilerParams(vmem_limit_bytes=56 * 1024 * 1024),
        cost_estimate=pl.CostEstimate(flops=3 * 10**9, bytes_accessed=12 * 10**6, transcendentals=0),
        name="back_hops",
    )(arrived, near, far, weight)


def forward_hops(hidden, diff_weight, table, pick):
    peers, channels, sensors = hidden.shape
    places = pick.shape[2]
    unit = to_lanes(jnp.eye(channels, dtype=jnp.bfloat16))
    one = to_lanes(diff_weight[:, channels : 2 * channels])
    two = to_lanes(diff_weight[:, 2 * channels :])
    return pl.pallas_call(
        functools.partial(forward_kernel, places),
        out_shape=jax.ShapeDtypeStruct(hidden.shape, jnp.bfloat16),
        in_specs=[VMEM] * 6,
        out_specs=VMEM,
        scratch_shapes=[
            pltpu.VMEM((peers, sensors, LANES), jnp.bfloat16),
            pltpu.VMEM((peers, sensors, LANES), jnp.bfloat16),
            pltpu.VMEM((peers // 2, 2, peers * CAPACITY, LANES), jnp.float32),
        ],
        compiler_params=pltpu.CompilerParams(vmem_limit_bytes=48 * 1024 * 1024),
        cost_estimate=pl.CostEstimate(flops=3 * 10**9, bytes_accessed=12 * 10**6, transcendentals=0),
        name="forward_hops",
    )(hidden, unit, one, two, table, pick)


def exchange(blocks, earlier=None):
    if earlier is not None:
        blocks, earlier = lax.optimization_barrier((blocks, earlier))
    return lax.all_to_all(blocks, "sensor", split_axis=0, concat_axis=0, tiled=True)


def per_device(
    signal,
    conv_weight,
    conv_bias,
    diff_weight,
    neighbour_index,
    neighbour_count,
    edge_weight,
    cotangent,
):
    channels, step_count, sensor_count = signal.shape
    peer_count = lax.axis_size("sensor")
    share_count = lax.axis_size("tm")

    graph = own_graph(
        peer_count,
        lax.axis_index("sensor"),
        lax.axis_index("tm"),
        neighbour_index,
        neighbour_count,
        edge_weight,
    )
    graph = jnp.broadcast_to(graph[None], (peer_count, 2 * SUBLANES, sensor_count))
    arrived = exchange(jnp.concatenate([cotangent.transpose(1, 0, 2), graph], axis=1))
    own = arrived[:, channels : channels + SUBLANES]
    near = [
        lax.ppermute(own, "tm", [(i, (i + by) % share_count) for i in range(share_count)])
        for by in range(2, share_count, 2)
    ]
    far = lax.ppermute(jnp.stack([own] + near), "tm", [(i, i ^ 1) for i in range(share_count)])

    tail_steps = signal[:, step_count - DILATION :, :]
    before = from_behind(tail_steps, "tm", 1)
    lagged = jnp.concatenate([before, signal[:, : step_count - DILATION, :]], axis=1)
    stacked = jnp.concatenate([lagged, signal], axis=0).reshape(
        2 * channels, step_count * sensor_count
    )
    preact = mm(conv_weight, stacked) + conv_bias[:, None]
    tanh_part = jnp.tanh(preact[:channels])
    gate_part = jax.nn.sigmoid(preact[channels:])
    hidden = (tanh_part * gate_part).astype(jnp.bfloat16)
    hidden_in = exchange(
        hidden.reshape(channels, step_count, sensor_count).transpose(1, 0, 2), arrived
    )

    back, table, pick = back_hops(arrived, jnp.stack(near), far, diff_weight)
    grad_out = exchange(back, hidden_in)
    mixed_out = exchange(forward_hops(hidden_in, diff_weight, table, pick), grad_out)

    theta_back = lax.dot_general(
        diff_weight[:, :channels],
        cotangent.reshape(channels, -1),
        COLUMNS_BY_COLUMNS,
        preferred_element_type=jnp.float32,
    )
    grad_hidden = theta_back + grad_out.transpose(1, 0, 2).reshape(channels, -1).astype(jnp.float32)
    grad_tanh = grad_hidden * gate_part * (1.0 - tanh_part * tanh_part)
    grad_gate = grad_hidden * tanh_part * gate_part * (1.0 - gate_part)
    grad_pre = jnp.concatenate([grad_tanh, grad_gate], axis=0).astype(jnp.bfloat16)
    conv_back = lax.dot_general(
        conv_weight, grad_pre, COLUMNS_BY_COLUMNS, preferred_element_type=jnp.float32
    )
    lag_back = conv_back[:channels].reshape(channels, step_count, sensor_count)
    now_back = conv_back[channels:].reshape(channels, step_count, sensor_count)
    after = from_behind(lag_back[:, :DILATION, :].astype(jnp.bfloat16), "tm", -1).astype(
        jnp.float32
    )
    shifted = jnp.concatenate([lag_back[:, DILATION:, :], after], axis=1)
    grad_signal = (cotangent.astype(jnp.float32) + now_back + shifted).astype(jnp.bfloat16)

    kept = signal.astype(jnp.float32) + mm(diff_weight[:, :channels], hidden).reshape(signal.shape)
    output = (kept + mixed_out.transpose(1, 0, 2).astype(jnp.float32)).astype(jnp.bfloat16)
    return (output, grad_signal)


def solution(mesh):
    placed = (
        P(None, "tm", "sensor"),
        P(),
        P(),
        P(),
        P("sensor", None),
        P("sensor"),
        P("sensor", None),
        P(None, "tm", "sensor"),
    )
    return jax.shard_map(
        per_device,
        mesh=mesh,
        in_specs=placed,
        out_specs=(P(None, "tm", "sensor"), P(None, "tm", "sensor")),
        check_vma=False,
    )
```

```python
import functools

import jax
import jax.numpy as jnp
from jax import lax
from jax.experimental import pallas as pl
from jax.experimental.pallas import tpu as pltpu
from jax.sharding import PartitionSpec as P

DILATION = 8
CAPACITY = 4
LANES = 128
SUBLANES = 8

ROWS_BY_ROWS = (((1,), (1,)), ((), ()))
COLUMNS_BY_COLUMNS = (((0,), (0,)), ((), ()))
VMEM = pl.BlockSpec(memory_space=pltpu.VMEM)


def from_behind(value, axis, by):
    count = lax.axis_size(axis)
    pairs = [(i, i + by) for i in range(count) if 0 <= i + by < count]
    return lax.ppermute(value, axis, pairs)


def mm(left, right):
    return jnp.dot(left, right, preferred_element_type=jnp.float32)


def mm_t(left, right):
    return lax.dot_general(left, right, ROWS_BY_ROWS, preferred_element_type=jnp.float32)


def t_mm(left, right):
    return lax.dot_general(left, right, COLUMNS_BY_COLUMNS, preferred_element_type=jnp.float32)


def graph_kernel(peers, me_ref, index_ref, count_ref, weight_ref, graph_ref, member_all, owner_all, rows_all):
    slots, sensors = index_ref.shape
    places = peers * CAPACITY
    half = (places + sensors) // 2
    me = me_ref[0]
    index = index_ref[...]
    live = lax.broadcasted_iota(jnp.int32, (slots, sensors), 0) < count_ref[...]
    masked = jnp.where(live, weight_ref[...], 0.0)
    trans = masked / jnp.sum(masked, axis=0, keepdims=True)
    owner = jnp.where(live, index // sensors, -1)
    member = index % sensors
    member_ids = lax.broadcasted_iota(jnp.int32, (sensors, sensors), 0)
    owner_ids = lax.broadcasted_iota(jnp.int32, (peers, sensors), 0)
    for j in range(slots):
        place = slice(j * sensors, (j + 1) * sensors)
        hit = member_ids == member[j : j + 1]
        member_all[:, place] = jnp.where(hit, 1.0, 0.0).astype(jnp.bfloat16)
        owner_all[:, place] = jnp.where(owner_ids == owner[j : j + 1], 1.0, 0.0).astype(jnp.bfloat16)
    named = mm_t(owner_all[...], member_all[...])
    named = (named > 0.0) & (owner_ids != me)
    flags = jnp.where(named, 1.0, 0.0).astype(jnp.bfloat16)
    below = lax.broadcasted_iota(jnp.int32, (sensors, sensors), 0) < lax.broadcasted_iota(
        jnp.int32, (sensors, sensors), 1
    )
    rank = mm(flags, jnp.where(below, 1.0, 0.0).astype(jnp.bfloat16))
    spread_rank = jnp.where(named, rank, 255.0).astype(jnp.bfloat16)
    ranks = mm(rank.astype(jnp.bfloat16), member_all[...])
    ranks = jnp.where(owner_all[...] > 0, ranks, 0.0)
    ranks = jnp.sum(ranks, axis=0, keepdims=True)
    ranks = jnp.concatenate([ranks[:, j * sensors : (j + 1) * sensors] for j in range(slots)], axis=0)
    distant = owner * CAPACITY + ranks.astype(jnp.int32)
    row = jnp.where(owner == me, places + member, distant) - half
    row = jnp.where(live, row, half)
    row = row.astype(jnp.float32)
    trans = trans.astype(jnp.bfloat16).astype(jnp.float32)
    part = SUBLANES // 2
    for i in range(slots // part):
        rows_all[i] = jnp.concatenate([row[i * part : (i + 1) * part], trans[i * part : (i + 1) * part]], axis=0)
    expand = lax.broadcasted_iota(jnp.int32, (places, peers), 0) // CAPACITY == lax.broadcasted_iota(
        jnp.int32, (places, peers), 1
    )
    spread_rank = mm(jnp.where(expand, 1.0, 0.0).astype(jnp.bfloat16), spread_rank)
    wanted_rank = (lax.broadcasted_iota(jnp.int32, (places, sensors), 0) % CAPACITY).astype(jnp.float32)
    chosen = jnp.where(spread_rank == wanted_rank, 1.0, 0.0).astype(jnp.bfloat16)
    lane_ids = lax.broadcasted_iota(jnp.int32, (SUBLANES, sensors), 1).astype(jnp.float32)
    first_row = lax.broadcasted_iota(jnp.int32, (SUBLANES, sensors), 0) == 0
    label = jnp.where(first_row, lane_ids, 1.0).astype(jnp.bfloat16)
    asked = mm_t(label, chosen)
    asked = jnp.where(asked[1:2] > 0.5, asked[0:1], -1.0)
    asked = [asked[:, i * sensors : (i + 1) * sensors] for i in range(places // sensors)]
    asked.append(jnp.zeros((SUBLANES - len(asked), sensors), jnp.float32))
    graph_ref[...] = jnp.concatenate([rows_all[me_ref[1]]] + asked, axis=0).astype(jnp.bfloat16)


def own_graph(peers, myself, share, index, count, weight):
    sensors, slots = index.shape
    return pl.pallas_call(
        functools.partial(graph_kernel, peers),
        out_shape=jax.ShapeDtypeStruct((2 * SUBLANES, sensors), jnp.bfloat16),
        in_specs=[pl.BlockSpec(memory_space=pltpu.SMEM), VMEM, VMEM, VMEM],
        out_specs=VMEM,
        scratch_shapes=[
            pltpu.VMEM((sensors, slots * sensors), jnp.bfloat16),
            pltpu.VMEM((peers, slots * sensors), jnp.bfloat16),
            pltpu.VMEM((2 * slots // SUBLANES, SUBLANES, sensors), jnp.float32),
        ],
        compiler_params=pltpu.CompilerParams(vmem_limit_bytes=32 * 1024 * 1024),
        cost_estimate=pl.CostEstimate(flops=4 * 10**8, bytes_accessed=10**6, transcendentals=0),
        name="own_graph",
    )(jnp.stack([myself, share]).astype(jnp.int32), index.T, count.reshape(1, sensors), weight.T)


def fill_tables(p, shares, asked_ref, table_ref, pick_ref):
    rows, sensors = table_ref.shape[1:]
    places = rows - sensors
    part = SUBLANES // 2
    chunk = 128
    codes = [share[j : j + 1, :] for share in shares for j in range(part)]
    weights = [share[part + j : part + j + 1, :] for share in shares for j in range(part)]
    blocks = []
    for start in range(0, rows, chunk):
        ids = lax.broadcasted_iota(jnp.int32, (chunk, sensors), 0).astype(jnp.float32) + (start - rows // 2)
        ids = ids.astype(jnp.bfloat16)
        total = jnp.zeros((chunk, sensors), jnp.bfloat16)
        for code, weight in zip(codes, weights):
            total = jnp.where(ids == code, weight, total)
        table_ref[p, start : start + chunk, :] = total
        blocks.append(total)
    own_ids = lax.broadcasted_iota(jnp.int32, (sensors, places), 0).astype(jnp.float32).astype(jnp.bfloat16)
    asked = asked_ref[pl.ds(p, 1), :].astype(jnp.bfloat16)
    one = jnp.ones((sensors, places), jnp.bfloat16)
    pick_ref[p] = jnp.where(own_ids == asked, one, jnp.zeros_like(one))
    return blocks[: places // chunk]


def turn_requests(requests, asked_ref):
    peers, sublanes, lanes = requests.shape
    places = peers * CAPACITY
    rows = lax.broadcasted_iota(jnp.int32, requests.shape, 1)
    parts = [jnp.sum(jnp.where(rows == i, requests, 0.0), axis=1) for i in range(places // lanes)]
    named = jnp.concatenate(parts, axis=1).astype(jnp.bfloat16)
    peer_ids = lax.broadcasted_iota(jnp.int32, (peers, places), 0)
    owner = lax.broadcasted_iota(jnp.int32, (peers, places), 1) // CAPACITY
    belongs = jnp.where(peer_ids == owner, 1.0, 0.0).astype(jnp.bfloat16)
    every = t_mm(named, belongs)
    same = lax.broadcasted_iota(jnp.int32, (places, places), 0) % CAPACITY
    same = same == lax.broadcasted_iota(jnp.int32, (places, places), 1) % CAPACITY
    asked_ref[...] = mm(belongs, jnp.where(same, every, 0.0).astype(jnp.bfloat16))


def swap_places(gathered, pair, left, right):
    count = left.shape[0]
    low = lax.broadcasted_iota(jnp.int32, left.shape, 0) % (2 * CAPACITY) < CAPACITY
    even = jnp.where(low, left, pltpu.roll(right, CAPACITY, 0))
    odd = jnp.where(low, pltpu.roll(left, count - CAPACITY, 0), right)
    at = pl.ds(pl.multiple_of(pair * 2 * CAPACITY, 2 * CAPACITY), 2 * CAPACITY)
    shape = (count // (2 * CAPACITY), 2 * CAPACITY, left.shape[1])
    gathered[:, 0, at, :] = even.reshape(shape)
    gathered[:, 1, at, :] = odd.reshape(shape)


def back_kernel(
    places, weight_ref, arrived_ref, far_ref, *refs
):
    near_refs = refs[:-8]
    out_ref, table_ref, pick_ref, base, second, first, gathered, asked = refs[-8:]
    peers, channels, sensors = out_ref.shape
    start = channels + SUBLANES
    turn_requests(arrived_ref[:, start:, :].astype(jnp.float32), asked)

    @pl.loop(0, peers // 2, unroll=4)
    def _(pair):
        sent = []
        for side in range(2):
            p = 2 * pair + side
            theta = t_mm(arrived_ref[p, :channels, :], weight_ref[...])
            base[p] = theta[:, :LANES]
            value = theta[:, LANES:].astype(jnp.bfloat16)
            second[p] = value
            shares = [arrived_ref[p, channels:start, :]]
            shares += [ref[p] for ref in near_refs]
            shares += [far_ref[i, p] for i in range(far_ref.shape[0])]
            blocks = fill_tables(p, shares, asked, table_ref, pick_ref)
            sent.append(jnp.concatenate([mm(block, value) for block in blocks], axis=0))
        swap_places(gathered, pair, *sent)

    def absorb(source, finish):
        @pl.loop(0, peers // 2, unroll=32)
        def _(pair):
            for side in range(2):
                p = 2 * pair + side
                far = mm(pick_ref[p], gathered[pair, side].astype(jnp.bfloat16))
                finish(p, far + mm(table_ref[p, places:, :], source[p]))

    def keep_first(p, value):
        first[p] = (base[p] + value).astype(jnp.bfloat16)

    def keep_out(p, value):
        out_ref[p] = value.T[:channels].astype(jnp.bfloat16)

    absorb(second, keep_first)

    @pl.loop(0, peers // 2, unroll=32)
    def _(pair):
        left = mm(table_ref[2 * pair, :places, :], first[2 * pair])
        right = mm(table_ref[2 * pair + 1, :places, :], first[2 * pair + 1])
        swap_places(gathered, pair, left, right)

    absorb(first, keep_out)


def forward_kernel(places, hidden_ref, unit_ref, one_ref, two_ref, table_ref, pick_ref, out_ref, start, middle, gathered):
    peers, channels, sensors = hidden_ref.shape

    @pl.loop(0, peers, unroll=32)
    def _(p):
        start[p] = t_mm(hidden_ref[p], unit_ref[...]).astype(jnp.bfloat16)

    def hop(source, finish):
        @pl.loop(0, peers // 2, unroll=32)
        def _(pair):
            left = t_mm(pick_ref[2 * pair], source[2 * pair])
            right = t_mm(pick_ref[2 * pair + 1], source[2 * pair + 1])
            swap_places(gathered, pair, left, right)

        @pl.loop(0, peers // 2, unroll=32)
        def _(pair):
            for side in range(2):
                p = 2 * pair + side
                far = t_mm(table_ref[p, :places, :], gathered[pair, side].astype(jnp.bfloat16))
                finish(p, (far + t_mm(table_ref[p, places:, :], source[p])).astype(jnp.bfloat16))

    def keep_middle(p, value):
        middle[p] = value

    def keep_out(p, value):
        mixed = mm_t(one_ref[...], middle[p]) + mm_t(two_ref[...], value)
        out_ref[p] = mixed.astype(jnp.bfloat16)

    hop(start, keep_middle)
    hop(middle, keep_out)


def to_lanes(block):
    return jnp.pad(block, ((0, 0), (0, LANES - block.shape[1])))


def back_hops(arrived, near, far, diff_weight):
    peers, _, sensors = arrived.shape
    channels = diff_weight.shape[0]
    places = peers * CAPACITY
    weight = jnp.concatenate(
        [to_lanes(diff_weight[:, channels : 2 * channels]), to_lanes(diff_weight[:, 2 * channels :])], axis=1
    )
    return pl.pallas_call(
        functools.partial(back_kernel, places),
        out_shape=(
            jax.ShapeDtypeStruct((peers, channels, sensors), jnp.bfloat16),
            jax.ShapeDtypeStruct((peers, places + sensors, sensors), jnp.bfloat16),
            jax.ShapeDtypeStruct((peers, sensors, places), jnp.bfloat16),
        ),
        in_specs=[VMEM] * (3 + len(near)),
        out_specs=(VMEM, VMEM, VMEM),
        scratch_shapes=[
            pltpu.VMEM((peers, sensors, LANES), jnp.float32),
            pltpu.VMEM((peers, sensors, LANES), jnp.bfloat16),
            pltpu.VMEM((peers, sensors, LANES), jnp.bfloat16),
            pltpu.VMEM((peers // 2, 2, peers * CAPACITY, LANES), jnp.float32),
            pltpu.VMEM((peers, places), jnp.float32),
        ],
        compiler_params=pltpu.CompilerParams(vmem_limit_bytes=56 * 1024 * 1024),
        cost_estimate=pl.CostEstimate(flops=3 * 10**9, bytes_accessed=12 * 10**6, transcendentals=0),
        name="back_hops",
    )(weight, arrived, far, *near)


def forward_hops(hidden, diff_weight, table, pick):
    peers, channels, sensors = hidden.shape
    places = pick.shape[2]
    unit = to_lanes(jnp.eye(channels, dtype=jnp.bfloat16))
    one = to_lanes(diff_weight[:, channels : 2 * channels])
    two = to_lanes(diff_weight[:, 2 * channels :])
    return pl.pallas_call(
        functools.partial(forward_kernel, places),
        out_shape=jax.ShapeDtypeStruct(hidden.shape, jnp.bfloat16),
        in_specs=[VMEM] * 6,
        out_specs=VMEM,
        scratch_shapes=[
            pltpu.VMEM((peers, sensors, LANES), jnp.bfloat16),
            pltpu.VMEM((peers, sensors, LANES), jnp.bfloat16),
            pltpu.VMEM((peers // 2, 2, peers * CAPACITY, LANES), jnp.float32),
        ],
        compiler_params=pltpu.CompilerParams(vmem_limit_bytes=48 * 1024 * 1024),
        cost_estimate=pl.CostEstimate(flops=3 * 10**9, bytes_accessed=12 * 10**6, transcendentals=0),
        name="forward_hops",
    )(hidden, unit, one, two, table, pick)


def finish_kernel(kept_ref, mixed_ref, out_ref, wide):
    channels, steps, sensors = kept_ref.shape
    for t in range(steps):
        wide[t * channels : (t + 1) * channels, :] = mixed_ref[t].astype(jnp.float32)
    for c in range(channels):
        mixed = wide[pl.ds(c, steps, stride=channels), :]
        out_ref[c] = (kept_ref[c] + mixed).astype(jnp.bfloat16)


def finish(kept, mixed):
    channels, steps, sensors = kept.shape
    return pl.pallas_call(
        finish_kernel,
        out_shape=jax.ShapeDtypeStruct(kept.shape, jnp.bfloat16),
        in_specs=[VMEM] * 2,
        out_specs=VMEM,
        scratch_shapes=[pltpu.VMEM((steps * channels, sensors), jnp.float32)],
        compiler_params=pltpu.CompilerParams(vmem_limit_bytes=32 * 1024 * 1024),
        cost_estimate=pl.CostEstimate(flops=10**6, bytes_accessed=4 * 10**6, transcendentals=0),
        name="finish",
    )(kept, mixed)


def exchange(blocks, earlier=None):
    if earlier is not None:
        blocks, earlier = lax.optimization_barrier((blocks, earlier))
    return lax.all_to_all(blocks, "sensor", split_axis=0, concat_axis=0, tiled=True)


def per_device(
    signal,
    conv_weight,
    conv_bias,
    diff_weight,
    neighbour_index,
    neighbour_count,
    edge_weight,
    cotangent,
):
    channels, step_count, sensor_count = signal.shape
    peer_count = lax.axis_size("sensor")
    share_count = lax.axis_size("tm")

    graph = own_graph(
        peer_count,
        lax.axis_index("sensor"),
        lax.axis_index("tm"),
        neighbour_index,
        neighbour_count,
        edge_weight,
    )
    graph_rows = SUBLANES + peer_count * CAPACITY // sensor_count
    graph = graph[:graph_rows].reshape(1, graph_rows // 2, 2, sensor_count)
    graph = jnp.broadcast_to(graph, (peer_count,) + graph.shape[1:])
    by_step = cotangent.transpose(1, 0, 2).reshape(peer_count, channels // 2, 2, sensor_count)
    pairs = exchange(jnp.concatenate([by_step, graph], axis=1))
    arrived = pairs.reshape(peer_count, channels + graph_rows, sensor_count)
    first_pair = channels // 2
    own = pairs[:, first_pair : first_pair + SUBLANES // 2].reshape(peer_count, SUBLANES, sensor_count)
    near = [
        lax.ppermute(own, "tm", [(i, (i + by) % share_count) for i in range(share_count)])
        for by in range(2, share_count, 2)
    ]
    far = lax.ppermute(jnp.stack([own] + near), "tm", [(i, i ^ 1) for i in range(share_count)])

    tail_steps = signal[:, step_count - DILATION :, :]
    before = from_behind(tail_steps, "tm", 1)
    lagged = jnp.concatenate([before, signal[:, : step_count - DILATION, :]], axis=1)
    stacked = jnp.concatenate([lagged, signal], axis=0).reshape(
        2 * channels, step_count * sensor_count
    )
    preact = mm(conv_weight, stacked) + conv_bias[:, None]
    tanh_part = jnp.tanh(preact[:channels])
    gate_part = jax.nn.sigmoid(preact[channels:])
    hidden = (tanh_part * gate_part).astype(jnp.bfloat16)
    hidden_in = exchange(
        hidden.reshape(channels, step_count, sensor_count).transpose(1, 0, 2), pairs
    )

    back, table, pick = back_hops(arrived, near, far, diff_weight)
    grad_out = exchange(back, hidden_in)
    mixed_out = exchange(forward_hops(hidden_in, diff_weight, table, pick), grad_out)

    theta_back = lax.dot_general(
        diff_weight[:, :channels],
        cotangent.reshape(channels, -1),
        COLUMNS_BY_COLUMNS,
        preferred_element_type=jnp.float32,
    )
    grad_hidden = theta_back + grad_out.transpose(1, 0, 2).reshape(channels, -1).astype(jnp.float32)
    grad_tanh = grad_hidden * gate_part * (1.0 - tanh_part * tanh_part)
    grad_gate = grad_hidden * tanh_part * gate_part * (1.0 - gate_part)
    grad_pre = jnp.concatenate([grad_tanh, grad_gate], axis=0).astype(jnp.bfloat16)
    conv_back = lax.dot_general(
        conv_weight, grad_pre, COLUMNS_BY_COLUMNS, preferred_element_type=jnp.float32
    )
    lag_back = conv_back[:channels].reshape(channels, step_count, sensor_count)
    now_back = conv_back[channels:].reshape(channels, step_count, sensor_count)
    after = from_behind(lag_back[:, :DILATION, :].astype(jnp.bfloat16), "tm", -1).astype(
        jnp.float32
    )
    shifted = jnp.concatenate([lag_back[:, DILATION:, :], after], axis=1)
    grad_signal = (cotangent.astype(jnp.float32) + now_back + shifted).astype(jnp.bfloat16)

    kept = signal.astype(jnp.float32) + mm(diff_weight[:, :channels], hidden).reshape(signal.shape)
    output = finish(kept, mixed_out)
    return (output, grad_signal)


def solution(mesh):
    placed = (
        P(None, "tm", "sensor"),
        P(),
        P(),
        P(),
        P("sensor", None),
        P("sensor"),
        P("sensor", None),
        P(None, "tm", "sensor"),
    )
    return jax.shard_map(
        per_device,
        mesh=mesh,
        in_specs=placed,
        out_specs=(P(None, "tm", "sensor"), P(None, "tm", "sensor")),
        check_vma=False,
    )
```
